128 devices in a mesh: sec: 8 (over x_hi, z), row: 16 (over x_lo, y, core).
Axes of the slice: x: 4 (x_hi: 2, x_lo: 2; x = x_hi * 2 + x_lo), y: 4, z: 4, core: 2. Of those that a mesh axis runs over, the one named last changes fastest.
Arguments:
- raw_sections: bfloat16 [8, 2048, 8192], P('sec', None, 'row'), may hold values from -6 to 6
- shift_rows: int32 [8, 16, 64], P('sec', 'row'), may hold values from -1 to 1
- source_cols: int32 [8, 16, 64], P('sec', 'row'), may hold values from 0 to 63
Outputs:
- vertical_scores: float32 [8, 3, 16, 64, 128], P('sec', None, 'row')
- horizontal_scores: float32 [8, 3, 16, 64, 128], P('sec', None, 'row')
The draws below stay inside these ranges and needn't reach their ends.
All inputs are finite; a program needn't handle non-finite values.
Results may differ from the reference program's by a relative error of at most 0.0003.
Values may be sent and summed in bfloat16 or wider, within the bound.
No kernel may reach another device: no remote copies, remote signals or barrier semaphores. Data moves between devices by JAX's collectives and lax.ppermute only.
A program may use at most 640 MiB of HBM per device.

```python
import jax
import jax.numpy as jnp
from jax import lax

W = 8192
BLOCK = 128
SECTIONS = 8
NB = 64
NBR = 16
H = 2048


def plant(array, own_key, least, high):
    shape = array.shape
    index_at = [jax.random.randint(jax.random.fold_in(own_key, axis), (), 0, shape[axis]) for axis in range(len(shape))]
    array = array.at[tuple(index_at)].set(least)
    longest = shape.index(max(shape))
    index_at[longest] = (index_at[longest] + 1) % shape[longest]
    return array.at[tuple(index_at)].set(high)


def steps_of(own_key, dims, pieces, smallest, top_value):
    def one(axis_at, shards_of):
        steps = jax.random.uniform(jax.random.fold_in(jax.random.fold_in(own_key, 6), axis_at), (shards_of,), jnp.float32, smallest / len(pieces), top_value / len(pieces))
        return jnp.repeat(jnp.exp(steps), dims[axis_at] // shards_of).reshape((-1,) + (1,) * (len(dims) - axis_at - 1))

    loudness = one(*pieces[0])
    for cut in pieces[1:]:
        loudness = loudness * one(*cut)
    return loudness


def centred(own_key, dims, spread, reach, pieces=(), kind=jnp.bfloat16):
    level = steps_of(own_key, dims, pieces, -0.22, 0.18) if pieces else 1.0
    values = jax.random.normal(own_key, dims, jnp.float32) * spread * level
    return jnp.minimum(jnp.maximum(values, -reach), reach).astype(kind)


def setup_inputs(seed: int = 0) -> dict:
    splits = jax.random.split(jax.random.key(seed), 4)
    return {
        "raw_sections": centred(splits[0], (SECTIONS, H, W), 1.0, 6.0, ((0, 8), (2, 16))),
        "shift_rows": plant(jax.random.randint(splits[1], (SECTIONS, NBR, NB), -1, 2), jax.random.fold_in(splits[1], 1), -1, 1).astype(jnp.int32),
        "source_cols": plant(jax.random.randint(splits[2], (SECTIONS, NBR, NB), 0, NB), jax.random.fold_in(splits[2], 1), 0, NB - 1).astype(jnp.int32),
    }


def lag_profile(matrix):
    block_len = matrix.shape[-1]
    leading = matrix.shape[:-2]
    doubled = jnp.concatenate([matrix, matrix], -1)
    flattened = doubled.reshape(leading + (2 * block_len * block_len,))
    flattened = jnp.pad(flattened, [(0, 0)] * len(leading) + [(0, block_len)])
    return flattened.reshape(leading + (block_len, 2 * block_len + 1))[..., :block_len].sum(-2)

def pair_scores(current, previous):
    current_f = current.astype(jnp.float32)
    previous_f = previous.astype(jnp.float32)
    row_corr = jnp.einsum('pjq,sjq->jps', current_f, previous_f, precision=lax.Precision.HIGHEST)
    col_corr = jnp.einsum('pjq,pjt->jqt', current_f, previous_f, precision=lax.Precision.HIGHEST)
    energy_a = lax.optimization_barrier(jnp.mean(current_f * current_f, axis=(0, 2)))
    energy_b = lax.optimization_barrier(jnp.mean(previous_f * previous_f, axis=(0, 2)))
    scaling = 1.0 / (BLOCK * jnp.sqrt(energy_a * energy_b + 1e-06))
    return (lag_profile(row_corr) * scaling[:, None], lag_profile(col_corr) * scaling[:, None])

def warp_section(section, shifts, columns):
    blocks = section.reshape(NBR, BLOCK, NB, BLOCK).transpose(0, 2, 1, 3)
    padded = jnp.pad(blocks, ((1, 1), (0, 0), (0, 0), (0, 0)))
    row_ids = jnp.arange(NBR, dtype=jnp.int32)[:, None] + 1 + shifts
    picked = padded[row_ids, columns]
    return picked.transpose(0, 2, 1, 3)

def reference(raw_sections, shift_rows, source_cols):
    warped = lax.map(lambda entry_tuple: warp_section(*entry_tuple), (raw_sections, shift_rows, source_cols))
    previous_list = []
    for offset in (1, 2, 3):
        zero_part = jnp.zeros((offset, NBR, BLOCK, NB, BLOCK), jnp.bfloat16)
        shifted = jnp.concatenate([zero_part, warped[:SECTIONS - offset]], 0)
        previous_list.append(shifted.reshape(SECTIONS * NBR, BLOCK, NB, BLOCK))
    current_all = warped.reshape(SECTIONS * NBR, BLOCK, NB, BLOCK)

    def score_entry(entry_tuple):
        current = entry_tuple[0]
        vertical_list = []
        horizontal_list = []
        for previous in entry_tuple[1:]:
            vertical, horizontal = pair_scores(current, previous)
            vertical_list.append(vertical)
            horizontal_list.append(horizontal)
        return (jnp.stack(vertical_list), jnp.stack(horizontal_list))
    vertical_all, horizontal_all = lax.map(score_entry, (current_all, previous_list[0], previous_list[1], previous_list[2]))
    vertical_all = vertical_all.reshape(SECTIONS, NBR, 3, NB, BLOCK).transpose(0, 2, 1, 3, 4)
    horizontal_all = horizontal_all.reshape(SECTIONS, NBR, 3, NB, BLOCK).transpose(0, 2, 1, 3, 4)
    return (vertical_all, horizontal_all)
```

```python
import functools

import jax
import jax.numpy as jnp
from jax import lax
from jax.experimental import pallas as pl
from jax.experimental.pallas import tpu as pltpu
from jax.sharding import PartitionSpec as P

BLOCK = 128
LAGS = 3


def warp_kernel(shifts, columns, up, own, down, out, sem):
    blocks = out.shape[0]
    width = own.shape[2] // BLOCK

    @pl.loop(0, blocks)
    def _(j):
        column = columns[j]
        stripe = column // width
        lane = pl.multiple_of((column % width) * BLOCK, BLOCK)
        shift = shifts[j]
        for step, source in ((-1, up), (0, own), (1, down)):

            @pl.when(shift == step)
            def _():
                pltpu.make_async_copy(
                    source.at[stripe, :, pl.ds(lane, BLOCK)], out.at[j], sem
                ).start()

    pltpu.make_async_copy(out, out, sem).wait()


def warp(shifts, columns, up, own, down):
    blocks = shifts.shape[0]
    return pl.pallas_call(
        warp_kernel,
        grid_spec=pltpu.PrefetchScalarGridSpec(
            num_scalar_prefetch=2,
            grid=(1,),
            in_specs=[pl.BlockSpec(memory_space=pl.ANY)] * 3,
            out_specs=pl.BlockSpec(memory_space=pl.ANY),
            scratch_shapes=[pltpu.SemaphoreType.DMA],
        ),
        out_shape=jax.ShapeDtypeStruct((blocks, BLOCK, BLOCK), jnp.bfloat16),
        name="warp",
    )(shifts, columns, up, own, down)


def lag_sums(matrix):
    total = matrix[0:8]
    for start in range(8, BLOCK, 8):
        total = total + pltpu.roll(matrix[start : start + 8], BLOCK - start, axis=1)
    for half in (4, 2, 1):
        upper = pltpu.roll(total, 8 - half, axis=0)
        total = total + pltpu.roll(upper, BLOCK - half, axis=1)
    return total[0:1]


def score_kernel(blocks, out, flipped):
    sections = blocks.shape[0]
    place = pl.ds(pl.program_id(0), 1)
    energies = []
    for s in range(sections):
        block = blocks[s, 0]
        flipped[s] = block.T
        values = block.astype(jnp.float32)
        energies.append(
            jnp.sum(jnp.sum(values * values, axis=0, keepdims=True), axis=1, keepdims=True)
            / (BLOCK * BLOCK)
        )
    for s in range(min(LAGS, sections)):
        for k in range(s + 1, LAGS + 1):
            out[s, 0, k - 1, place, :] = jnp.zeros((1, BLOCK), jnp.float32)
            out[s, 1, k - 1, place, :] = jnp.zeros((1, BLOCK), jnp.float32)
    for back in range(sections - 1):
        count = min(LAGS, sections - 1 - back)
        previous = blocks[back, 0]
        current = blocks[back + 1 : back + 1 + count, 0].reshape(count * BLOCK, BLOCK)
        current_flipped = flipped[back + 1 : back + 1 + count].reshape(count * BLOCK, BLOCK)
        row_corr = jnp.dot(current, flipped[back], preferred_element_type=jnp.float32)
        col_corr = jnp.dot(current_flipped, previous, preferred_element_type=jnp.float32)
        for k in range(1, count + 1):
            s = back + k
            scaling = 1.0 / (BLOCK * jnp.sqrt(energies[s] * energies[back] + 1e-06))
            part = slice((k - 1) * BLOCK, k * BLOCK)
            out[s, 0, k - 1, place, :] = lag_sums(row_corr[part]) * scaling
            out[s, 1, k - 1, place, :] = lag_sums(col_corr[part]) * scaling


def scores(blocks):
    sections, columns = blocks.shape[:2]
    shape = (sections, 2, LAGS, columns, BLOCK)
    pairs = LAGS * sections - LAGS * (LAGS + 1) // 2
    return pl.pallas_call(
        score_kernel,
        grid=(columns,),
        in_specs=[pl.BlockSpec((sections, 1, BLOCK, BLOCK), lambda j: (0, j, 0, 0))],
        out_specs=pl.BlockSpec(shape, lambda j: (0, 0, 0, 0, 0)),
        out_shape=jax.ShapeDtypeStruct(shape, jnp.float32),
        scratch_shapes=[pltpu.VMEM((sections, BLOCK, BLOCK), jnp.bfloat16)],
        compiler_params=pltpu.CompilerParams(vmem_limit_bytes=32 * 1024 * 1024),
        cost_estimate=pl.CostEstimate(
            flops=4 * columns * pairs * BLOCK**3, bytes_accessed=2 * blocks.size, transcendentals=0
        ),
        name="scores",
    )(blocks)


def body(raw_sections, shift_rows, source_cols):
    raw = raw_sections[0]
    rows = lax.axis_size("row")
    sections = lax.axis_size("sec")
    stripes = lax.all_to_all(
        raw.reshape(rows, -1, raw.shape[1]), "row", split_axis=0, concat_axis=0, tiled=True
    )
    forward = [(i, i + 1) for i in range(rows - 1)]
    backward = [(target, source) for source, target in forward]
    up = lax.ppermute(stripes, "row", forward)
    down = lax.ppermute(stripes, "row", backward)
    warped = warp(shift_rows[0, 0], source_cols[0, 0], up, stripes, down)
    warped = warped.reshape(sections, -1, BLOCK, BLOCK)
    chunk = lax.all_to_all(warped, "sec", split_axis=0, concat_axis=0, tiled=True)
    result = scores(chunk)
    result = lax.all_to_all(result, "sec", split_axis=0, concat_axis=0, tiled=True)
    result = result.transpose(1, 2, 0, 3, 4).reshape(2, 1, LAGS, 1, -1, BLOCK)
    return result[0], result[1]


def solution(mesh):
    return jax.shard_map(
        body,
        mesh=mesh,
        in_specs=(P("sec", None, "row"), P("sec", "row", None), P("sec", "row", None)),
        out_specs=(P("sec", None, "row", None, None), P("sec", None, "row", None, None)),
        check_vma=False,
    )
```

```python
import functools

import jax
import jax.numpy as jnp
from jax import lax
from jax.experimental import pallas as pl
from jax.experimental.pallas import tpu as pltpu
from jax.sharding import PartitionSpec as P

BLOCK = 128
LAGS = 3


def warp_kernel(shifts, columns, up, own, down, out):
    width = own.shape[2] // BLOCK

    @pl.loop(0, out.shape[0], unroll=4)
    def _(j):
        column = columns[j]
        stripe = column // width
        lane = pl.multiple_of((column % width) * BLOCK, BLOCK)
        shift = shifts[j]
        for step, source in ((-1, up), (0, own), (1, down)):

            @pl.when(shift == step)
            def _():
                out[j] = source[stripe, :, pl.ds(lane, BLOCK)]


def warp(shifts, columns, up, own, down):
    shape = (shifts.shape[0], BLOCK, BLOCK)
    return pl.pallas_call(
        warp_kernel,
        in_specs=[pl.BlockSpec(memory_space=pltpu.SMEM)] * 2
        + [pl.BlockSpec(memory_space=pltpu.VMEM)] * 3,
        out_specs=pl.BlockSpec(memory_space=pltpu.VMEM),
        out_shape=jax.ShapeDtypeStruct(shape, jnp.bfloat16),
        compiler_params=pltpu.CompilerParams(vmem_limit_bytes=16 * 1024 * 1024),
        cost_estimate=pl.CostEstimate(
            flops=0, bytes_accessed=8 * own.size, transcendentals=0
        ),
        name="warp",
    )(shifts, columns, up, own, down)


def partial_lags(matrix):
    total = matrix[0:8]
    for start in range(8, matrix.shape[0], 8):
        total = total + pltpu.roll(matrix[start : start + 8], BLOCK - start, axis=1)
    return total


def halves(block):
    return jnp.concatenate([block[: BLOCK // 2], block[BLOCK // 2 :]], axis=1)


def turned(block):
    return jnp.concatenate([block[BLOCK // 2 :], block[: BLOCK // 2]], axis=0)


def score_kernel(blocks, out, flipped, by_row, by_column, lags, squares):
    sections = blocks.shape[0]
    steps = out.shape[3]
    place = pl.ds(pl.multiple_of(pl.program_id(0) * 8, 8), 8)
    for s in range(sections):
        block = blocks[s, 0]
        flip = block.T
        flipped[s] = flip
        by_row[s, :BLOCK] = flip
        by_row[s, BLOCK:] = turned(block).T
        by_column[s, :BLOCK] = block
        by_column[s, BLOCK:] = pltpu.roll(block, BLOCK // 2, axis=1)
        values = block.astype(jnp.float32)
        values = values * values
        total = values[0:8]
        for start in range(8, BLOCK, 8):
            total = total + values[start : start + 8]
        squares[s, place, :] = total
    for back in range(sections - 1):
        count = min(LAGS, sections - 1 - back)
        near = range(back + 1, back + 1 + count)
        current = jnp.concatenate([halves(blocks[s, 0]) for s in near], axis=0)
        current_flipped = jnp.concatenate([halves(flipped[s]) for s in near], axis=0)
        row_corr = jnp.dot(current, by_row[back], preferred_element_type=jnp.float32)
        col_corr = jnp.dot(current_flipped, by_column[back], preferred_element_type=jnp.float32)
        for k in range(count):
            part = slice(k * BLOCK // 2, (k + 1) * BLOCK // 2)
            lags[back + 1 + k, 0, k, place, :] = partial_lags(row_corr[part])
            lags[back + 1 + k, 1, k, place, :] = partial_lags(col_corr[part])

    @pl.when(pl.program_id(0) == steps - 1)
    def _():
        energies = []
        for s in range(sections):
            total = squares[s, pl.ds(0, steps, stride=8), :]
            for b in range(1, 8):
                total = total + squares[s, pl.ds(b, steps, stride=8), :]
            energies.append(jnp.sum(total, axis=1, keepdims=True) / (BLOCK * BLOCK))
        for s in range(sections):
            for k in range(1, LAGS + 1):
                if s < k:
                    for way in range(2):
                        out[s, way, k - 1] = jnp.zeros((steps, BLOCK), jnp.float32)
                    continue
                scaling = 1.0 / (BLOCK * jnp.sqrt(energies[s] * energies[s - k] + 1e-06))
                for way in range(2):
                    total = lags[s, way, k - 1, pl.ds(0, steps, stride=8), :]
                    for b in range(1, 8):
                        row = lags[s, way, k - 1, pl.ds(b, steps, stride=8), :]
                        total = total + pltpu.roll(row, BLOCK - b, axis=1)
                    out[s, way, k - 1] = total * scaling


def scores(blocks):
    sections, columns = blocks.shape[:2]
    shape = (sections, 2, LAGS, columns, BLOCK)
    pairs = LAGS * sections - LAGS * (LAGS + 1) // 2
    return pl.pallas_call(
        score_kernel,
        grid=(columns,),
        in_specs=[pl.BlockSpec((sections, 1, BLOCK, BLOCK), lambda j: (0, j, 0, 0))],
        out_specs=pl.BlockSpec(shape, lambda j: (0, 0, 0, 0, 0)),
        out_shape=jax.ShapeDtypeStruct(shape, jnp.float32),
        scratch_shapes=[
            pltpu.VMEM((sections, BLOCK, BLOCK), jnp.bfloat16),
            pltpu.VMEM((sections, 2 * BLOCK, BLOCK), jnp.bfloat16),
            pltpu.VMEM((sections, 2 * BLOCK, BLOCK), jnp.bfloat16),
            pltpu.VMEM((sections, 2, LAGS, columns * 8, BLOCK), jnp.float32),
            pltpu.VMEM((sections, columns * 8, BLOCK), jnp.float32),
        ],
        compiler_params=pltpu.CompilerParams(vmem_limit_bytes=16 * 1024 * 1024),
        cost_estimate=pl.CostEstimate(
            flops=4 * columns * pairs * BLOCK**3, bytes_accessed=2 * blocks.size, transcendentals=0
        ),
        name="scores",
    )(blocks)


def body(raw_sections, shift_rows, source_cols):
    raw = raw_sections[0]
    rows = lax.axis_size("row")
    sections = lax.axis_size("sec")
    stripes = lax.all_to_all(
        raw.reshape(rows, -1, raw.shape[1]), "row", split_axis=0, concat_axis=0, tiled=True
    )
    forward = [(i, i + 1) for i in range(rows - 1)]
    backward = [(target, source) for source, target in forward]
    up = lax.ppermute(stripes, "row", forward)
    down = lax.ppermute(stripes, "row", backward)
    warped = warp(shift_rows[0, 0], source_cols[0, 0], up, stripes, down)
    warped = warped.reshape(sections, -1, BLOCK, BLOCK)
    chunk = lax.all_to_all(warped, "sec", split_axis=0, concat_axis=0, tiled=True)
    result = scores(chunk)
    result = lax.all_to_all(result, "sec", split_axis=0, concat_axis=0, tiled=True)
    result = result.transpose(1, 2, 0, 3, 4).reshape(2, 1, LAGS, 1, -1, BLOCK)
    return result[0], result[1]


def solution(mesh):
    return jax.shard_map(
        body,
        mesh=mesh,
        in_specs=(P("sec", None, "row"), P("sec", "row", None), P("sec", "row", None)),
        out_specs=(P("sec", None, "row", None, None), P("sec", None, "row", None, None)),
        check_vma=False,
    )
```

```python
import functools

import jax
import jax.numpy as jnp
from jax import lax
from jax.experimental import pallas as pl
from jax.experimental.pallas import tpu as pltpu
from jax.sharding import PartitionSpec as P

BLOCK = 128
LAGS = 3


def warp_kernel(shifts, columns, own, beside, across, out):
    width = own.shape[2] // BLOCK
    toward = 2 * lax.rem(lax.axis_index("row"), 2) - 1

    @pl.loop(0, out.shape[0], unroll=4)
    def _(j):
        column = columns[j]
        stripe = column // width
        lane = pl.multiple_of((column % width) * BLOCK, BLOCK)
        side = shifts[j] * toward
        for at, source in ((0, own), (-1, beside), (1, across)):

            @pl.when(side == at)
            def _():
                out[j] = source[stripe, :, pl.ds(lane, BLOCK)]


def warp(shifts, columns, own, beside, across):
    shape = (shifts.shape[0], BLOCK, BLOCK)
    return pl.pallas_call(
        warp_kernel,
        in_specs=[pl.BlockSpec(memory_space=pltpu.SMEM)] * 2
        + [pl.BlockSpec(memory_space=pltpu.VMEM)] * 3,
        out_specs=pl.BlockSpec(memory_space=pltpu.VMEM),
        out_shape=jax.ShapeDtypeStruct(shape, jnp.bfloat16),
        compiler_params=pltpu.CompilerParams(vmem_limit_bytes=16 * 1024 * 1024),
        cost_estimate=pl.CostEstimate(
            flops=0, bytes_accessed=8 * own.size, transcendentals=0
        ),
        name="warp",
    )(shifts, columns, own, beside, across)


def partial_lags(matrix):
    total = matrix[0:8]
    for start in range(8, matrix.shape[0], 8):
        total = total + pltpu.roll(matrix[start : start + 8], BLOCK - start, axis=1)
    return total


def halves(block):
    return jnp.concatenate([block[: BLOCK // 2], block[BLOCK // 2 :]], axis=1)


def turned(block):
    return jnp.concatenate([block[BLOCK // 2 :], block[: BLOCK // 2]], axis=0)


def score_kernel(blocks, out, flipped, by_row, by_column, lags, squares):
    sections = blocks.shape[0]
    steps = out.shape[3]
    place = pl.ds(pl.multiple_of(pl.program_id(0) * 8, 8), 8)
    for s in range(sections):
        block = blocks[s, 0]
        flip = block.T
        flipped[s] = flip
        by_row[s, :BLOCK] = flip
        by_row[s, BLOCK:] = turned(block).T
        by_column[s, :BLOCK] = block
        by_column[s, BLOCK:] = pltpu.roll(block, BLOCK // 2, axis=1)
        values = block.astype(jnp.float32)
        values = values * values
        total = values[0:8]
        for start in range(8, BLOCK, 8):
            total = total + values[start : start + 8]
        squares[s, place, :] = total
    for back in range(sections - 1):
        count = min(LAGS, sections - 1 - back)
        near = range(back + 1, back + 1 + count)
        current = jnp.concatenate([halves(blocks[s, 0]) for s in near], axis=0)
        current_flipped = jnp.concatenate([halves(flipped[s]) for s in near], axis=0)
        row_corr = jnp.dot(current, by_row[back], preferred_element_type=jnp.float32)
        col_corr = jnp.dot(current_flipped, by_column[back], preferred_element_type=jnp.float32)
        for k in range(count):
            part = slice(k * BLOCK // 2, (k + 1) * BLOCK // 2)
            lags[back + 1 + k, 0, k, place, :] = partial_lags(row_corr[part])
            lags[back + 1 + k, 1, k, place, :] = partial_lags(col_corr[part])

    @pl.when(pl.program_id(0) == steps - 1)
    def _():
        energies = []
        for s in range(sections):
            total = squares[s, pl.ds(0, steps, stride=8), :]
            for b in range(1, 8):
                total = total + squares[s, pl.ds(b, steps, stride=8), :]
            energies.append(jnp.sum(total, axis=1, keepdims=True) / (BLOCK * BLOCK))
        for s in range(sections):
            for k in range(1, LAGS + 1):
                if s < k:
                    for way in range(2):
                        out[s, way, k - 1] = jnp.zeros((steps, BLOCK), jnp.float32)
                    continue
                scaling = 1.0 / (BLOCK * jnp.sqrt(energies[s] * energies[s - k] + 1e-06))
                for way in range(2):
                    total = lags[s, way, k - 1, pl.ds(0, steps, stride=8), :]
                    for b in range(1, 8):
                        row = lags[s, way, k - 1, pl.ds(b, steps, stride=8), :]
                        total = total + pltpu.roll(row, BLOCK - b, axis=1)
                    out[s, way, k - 1] = total * scaling


def scores(blocks):
    sections, columns = blocks.shape[:2]
    shape = (sections, 2, LAGS, columns, BLOCK)
    pairs = LAGS * sections - LAGS * (LAGS + 1) // 2
    return pl.pallas_call(
        score_kernel,
        grid=(columns,),
        in_specs=[pl.BlockSpec((sections, 1, BLOCK, BLOCK), lambda j: (0, j, 0, 0))],
        out_specs=pl.BlockSpec(shape, lambda j: (0, 0, 0, 0, 0)),
        out_shape=jax.ShapeDtypeStruct(shape, jnp.float32),
        scratch_shapes=[
            pltpu.VMEM((sections, BLOCK, BLOCK), jnp.bfloat16),
            pltpu.VMEM((sections, 2 * BLOCK, BLOCK), jnp.bfloat16),
            pltpu.VMEM((sections, 2 * BLOCK, BLOCK), jnp.bfloat16),
            pltpu.VMEM((sections, 2, LAGS, columns * 8, BLOCK), jnp.float32),
            pltpu.VMEM((sections, columns * 8, BLOCK), jnp.float32),
        ],
        compiler_params=pltpu.CompilerParams(vmem_limit_bytes=16 * 1024 * 1024),
        cost_estimate=pl.CostEstimate(
            flops=4 * columns * pairs * BLOCK**3, bytes_accessed=2 * blocks.size, transcendentals=0
        ),
        name="scores",
    )(blocks)


def body(raw_sections, shift_rows, source_cols):
    raw = raw_sections[0]
    rows = lax.axis_size("row")
    sections = lax.axis_size("sec")
    own = lax.all_to_all(
        raw.reshape(rows, BLOCK, raw.shape[1]), "row", split_axis=0, concat_axis=0, tiled=True
    )
    chips = rows // 2
    links = [(2 * r, 2 * r - 1) for r in range(1, chips)]
    links += [(2 * r + 1, 2 * r + 2) for r in range(chips - 1)]
    across = lax.ppermute(own, "row", links)
    beside = lax.ppermute(own, "row", [(i, i ^ 1) for i in range(rows)])
    warped = warp(shift_rows[0, 0], source_cols[0, 0], own, beside, across)
    warped = warped.reshape(sections, -1, BLOCK, BLOCK)
    chunk = lax.all_to_all(warped, "sec", split_axis=0, concat_axis=0, tiled=True)
    result = scores(chunk)
    result = lax.all_to_all(result, "sec", split_axis=0, concat_axis=0, tiled=True)
    result = result.transpose(1, 2, 0, 3, 4).reshape(2, 1, LAGS, 1, -1, BLOCK)
    return result[0], result[1]


def solution(mesh):
    return jax.shard_map(
        body,
        mesh=mesh,
        in_specs=(P("sec", None, "row"), P("sec", "row", None), P("sec", "row", None)),
        out_specs=(P("sec", None, "row", None, None), P("sec", None, "row", None, None)),
        check_vma=False,
    )
```

```python
import functools

import jax
import jax.numpy as jnp
from jax import lax
from jax.experimental import pallas as pl
from jax.experimental.pallas import tpu as pltpu
from jax.sharding import PartitionSpec as P

BLOCK = 128
LAGS = 3
GROUP = 2


def warp_kernel(shifts, columns, own, beside, across, out):
    width = own.shape[2] // BLOCK
    toward = 2 * lax.rem(lax.axis_index("row"), 2) - 1

    @pl.loop(0, out.shape[0], unroll=8)
    def _(j):
        column = columns[j]
        stripe = lax.div(column, width)
        lane = pl.multiple_of(lax.rem(column, width) * BLOCK, BLOCK)
        side = shifts[j] * toward
        here = own[stripe, :, pl.ds(lane, BLOCK)]
        low = beside[stripe, :, pl.ds(lane, BLOCK)]
        high = across[stripe, :, pl.ds(lane, BLOCK)]
        out[j] = jnp.where(side == 0, here, jnp.where(side == 1, high, low))


def warp(shifts, columns, own, beside, across):
    shape = (shifts.shape[0], BLOCK, BLOCK)
    return pl.pallas_call(
        warp_kernel,
        in_specs=[pl.BlockSpec(memory_space=pltpu.SMEM)] * 2
        + [pl.BlockSpec(memory_space=pltpu.VMEM)] * 3,
        out_specs=pl.BlockSpec(memory_space=pltpu.VMEM),
        out_shape=jax.ShapeDtypeStruct(shape, jnp.bfloat16),
        compiler_params=pltpu.CompilerParams(vmem_limit_bytes=16 * 1024 * 1024),
        cost_estimate=pl.CostEstimate(
            flops=0, bytes_accessed=8 * own.size, transcendentals=0
        ),
        name="warp",
    )(shifts, columns, own, beside, across)


def partial_lags(matrix):
    total = matrix[0:8]
    for start in range(8, matrix.shape[0], 8):
        total = total + pltpu.roll(matrix[start : start + 8], BLOCK - start, axis=1)
    return total


def halves(block):
    return jnp.concatenate([block[: BLOCK // 2], block[BLOCK // 2 :]], axis=1)


def turned(block):
    return jnp.concatenate([block[BLOCK // 2 :], block[: BLOCK // 2]], axis=0)


def score_kernel(blocks, out, flipped, by_column, lags, squares):
    sections, group = blocks.shape[:2]
    steps = out.shape[3]
    for column in range(group):
        place = pl.ds(pl.multiple_of((pl.program_id(0) * group + column) * 8, 8), 8)
        by_row = []
        for s in range(sections):
            block = blocks[s, column]
            by_row.append(jnp.concatenate([block, turned(block)], axis=1))
            flipped[s] = block.T
            by_column[s, :BLOCK] = block
            by_column[s, BLOCK:] = pltpu.roll(block, BLOCK // 2, axis=1)
            values = block.astype(jnp.float32)
            values = values * values
            total = values[0:8]
            for start in range(8, BLOCK, 8):
                total = total + values[start : start + 8]
            squares[s, place, :] = total
        for back in range(sections - 1):
            count = min(LAGS, sections - 1 - back)
            near = range(back + 1, back + 1 + count)
            current = jnp.concatenate([halves(blocks[s, column]) for s in near], axis=0)
            current_flipped = jnp.concatenate([halves(flipped[s]) for s in near], axis=0)
            row_corr = lax.dot_general(
                current, by_row[back], (((1,), (1,)), ((), ())), preferred_element_type=jnp.float32
            )
            col_corr = jnp.dot(
                current_flipped, by_column[back], preferred_element_type=jnp.float32
            )
            for k in range(count):
                part = slice(k * BLOCK // 2, (k + 1) * BLOCK // 2)
                lags[back + 1 + k, 0, k, place, :] = partial_lags(row_corr[part])
                lags[back + 1 + k, 1, k, place, :] = partial_lags(col_corr[part])

    @pl.when(pl.program_id(0) == pl.num_programs(0) - 1)
    def _():
        energies = []
        for s in range(sections):
            total = squares[s, pl.ds(0, steps, stride=8), :]
            for b in range(1, 8):
                total = total + squares[s, pl.ds(b, steps, stride=8), :]
            energies.append(jnp.sum(total, axis=1, keepdims=True) / (BLOCK * BLOCK))
        for s in range(sections):
            for k in range(1, LAGS + 1):
                if s < k:
                    for way in range(2):
                        out[s, way, k - 1] = jnp.zeros((steps, BLOCK), jnp.float32)
                    continue
                scaling = 1.0 / (BLOCK * jnp.sqrt(energies[s] * energies[s - k] + 1e-06))
                for way in range(2):
                    total = lags[s, way, k - 1, pl.ds(0, steps, stride=8), :]
                    for b in range(1, 8):
                        row = lags[s, way, k - 1, pl.ds(b, steps, stride=8), :]
                        total = total + pltpu.roll(row, BLOCK - b, axis=1)
                    out[s, way, k - 1] = total * scaling


def scores(blocks):
    sections, columns = blocks.shape[:2]
    shape = (sections, 2, LAGS, columns, BLOCK)
    pairs = LAGS * sections - LAGS * (LAGS + 1) // 2
    return pl.pallas_call(
        score_kernel,
        grid=(columns // GROUP,),
        in_specs=[pl.BlockSpec((sections, GROUP, BLOCK, BLOCK), lambda j: (0, j, 0, 0))],
        out_specs=pl.BlockSpec(shape, lambda j: (0, 0, 0, 0, 0)),
        out_shape=jax.ShapeDtypeStruct(shape, jnp.float32),
        scratch_shapes=[
            pltpu.VMEM((sections, BLOCK, BLOCK), jnp.bfloat16),
            pltpu.VMEM((sections, 2 * BLOCK, BLOCK), jnp.bfloat16),
            pltpu.VMEM((sections, 2, LAGS, columns * 8, BLOCK), jnp.float32),
            pltpu.VMEM((sections, columns * 8, BLOCK), jnp.float32),
        ],
        compiler_params=pltpu.CompilerParams(vmem_limit_bytes=16 * 1024 * 1024),
        cost_estimate=pl.CostEstimate(
            flops=4 * columns * pairs * BLOCK**3, bytes_accessed=2 * blocks.size, transcendentals=0
        ),
        name="scores",
    )(blocks)


def body(raw_sections, shift_rows, source_cols):
    raw = raw_sections[0]
    rows = lax.axis_size("row")
    sections = lax.axis_size("sec")
    own = lax.all_to_all(
        raw.reshape(rows, BLOCK, raw.shape[1]), "row", split_axis=0, concat_axis=0, tiled=True
    )
    chips = rows // 2
    links = [(2 * r, 2 * r - 1) for r in range(1, chips)]
    links += [(2 * r + 1, 2 * r + 2) for r in range(chips - 1)]
    across = lax.ppermute(own, "row", links)
    beside = lax.ppermute(own, "row", [(i, i ^ 1) for i in range(rows)])
    warped = warp(shift_rows[0, 0], source_cols[0, 0], own, beside, across)
    warped = warped.reshape(sections, -1, BLOCK, BLOCK)
    chunk = lax.all_to_all(warped, "sec", split_axis=0, concat_axis=0, tiled=True)
    result = scores(chunk)
    result = lax.all_to_all(result, "sec", split_axis=0, concat_axis=0, tiled=True)
    result = result.transpose(1, 2, 0, 3, 4).reshape(2, 1, LAGS, 1, -1, BLOCK)
    return result[0], result[1]


def solution(mesh):
    return jax.shard_map(
        body,
        mesh=mesh,
        in_specs=(P("sec", None, "row"), P("sec", "row", None), P("sec", "row", None)),
        out_specs=(P("sec", None, "row", None, None), P("sec", None, "row", None, None)),
        check_vma=False,
    )
```

```python
import functools

import jax
import jax.numpy as jnp
from jax import lax
from jax.experimental import pallas as pl
from jax.experimental.pallas import tpu as pltpu
from jax.sharding import PartitionSpec as P

BLOCK = 128
LAGS = 3


def warp_kernel(shifts, columns, own, beside, across, out):
    width = own.shape[2] // BLOCK
    toward = 2 * lax.rem(lax.axis_index("row"), 2) - 1

    @pl.loop(0, out.shape[0], unroll=8)
    def _(j):
        column = columns[j]
        stripe = lax.div(column, width)
        lane = pl.multiple_of(lax.rem(column, width) * BLOCK, BLOCK)
        side = shifts[j] * toward
        here = own[stripe, :, pl.ds(lane, BLOCK)]
        low = beside[stripe, :, pl.ds(lane, BLOCK)]
        high = across[stripe, :, pl.ds(lane, BLOCK)]
        out[j] = jnp.where(side == 0, here, jnp.where(side == 1, high, low))


def warp(shifts, columns, own, beside, across):
    shape = (shifts.shape[0], BLOCK, BLOCK)
    return pl.pallas_call(
        warp_kernel,
        in_specs=[pl.BlockSpec(memory_space=pltpu.SMEM)] * 2
        + [pl.BlockSpec(memory_space=pltpu.VMEM)] * 3,
        out_specs=pl.BlockSpec(memory_space=pltpu.VMEM),
        out_shape=jax.ShapeDtypeStruct(shape, jnp.bfloat16),
        compiler_params=pltpu.CompilerParams(vmem_limit_bytes=16 * 1024 * 1024),
        cost_estimate=pl.CostEstimate(
            flops=0, bytes_accessed=8 * own.size, transcendentals=0
        ),
        name="warp",
    )(shifts, columns, own, beside, across)


def partial_lags(matrix):
    total = matrix[0:8]
    for start in range(8, matrix.shape[0], 8):
        total = total + pltpu.roll(matrix[start : start + 8], BLOCK - start, axis=1)
    return total


def halves(block):
    return jnp.concatenate([block[: BLOCK // 2], block[BLOCK // 2 :]], axis=1)


def turned(block):
    half = BLOCK // 2
    return jnp.concatenate([block, jnp.concatenate([block[half:], block[:half]], axis=0)], axis=1)


def along_lanes(left, right):
    return lax.dot_general(
        left, right, (((1,), (1,)), ((), ())), preferred_element_type=jnp.float32
    )


def score_kernel(blocks, out, flipped, lags, squares):
    sections, columns = blocks.shape[:2]
    half = BLOCK // 2
    for column in range(columns):
        place = slice(column * 8, (column + 1) * 8)
        for s in range(sections):
            block = blocks[s, column]
            flipped[s] = block.T
            values = block.astype(jnp.float32)
            values = values * values
            total = values[0:8]
            for start in range(8, BLOCK, 8):
                total = total + values[start : start + 8]
            squares[s, place, :] = total
        for back in range(sections - 1):
            count = min(LAGS, sections - 1 - back)
            near = range(back + 1, back + 1 + count)
            current = jnp.concatenate([halves(blocks[s, column]) for s in near], axis=0)
            current_flipped = jnp.concatenate([halves(flipped[s]) for s in near], axis=0)
            row_corr = along_lanes(current, turned(blocks[back, column]))
            col_corr = along_lanes(current_flipped, turned(flipped[back]))
            for k in range(count):
                part = slice(k * half, (k + 1) * half)
                lags[back + 1 + k, 0, k, place, :] = partial_lags(row_corr[part])
                lags[back + 1 + k, 1, k, place, :] = partial_lags(col_corr[part])
    energies = []
    for s in range(sections):
        total = squares[s, pl.ds(0, columns, stride=8), :]
        for b in range(1, 8):
            total = total + squares[s, pl.ds(b, columns, stride=8), :]
        energies.append(jnp.sum(total, axis=1, keepdims=True) / (BLOCK * BLOCK))
    for s in range(sections):
        for k in range(1, LAGS + 1):
            if s < k:
                for way in range(2):
                    out[s, way, k - 1] = jnp.zeros((columns, BLOCK), jnp.float32)
                continue
            scaling = 1.0 / (BLOCK * jnp.sqrt(energies[s] * energies[s - k] + 1e-06))
            for way in range(2):
                total = lags[s, way, k - 1, pl.ds(0, columns, stride=8), :]
                for b in range(1, 8):
                    row = lags[s, way, k - 1, pl.ds(b, columns, stride=8), :]
                    total = total + pltpu.roll(row, BLOCK - b, axis=1)
                out[s, way, k - 1] = total * scaling


def scores(blocks):
    sections, columns = blocks.shape[:2]
    shape = (sections, 2, LAGS, columns, BLOCK)
    pairs = LAGS * sections - LAGS * (LAGS + 1) // 2
    return pl.pallas_call(
        score_kernel,
        in_specs=[pl.BlockSpec(memory_space=pltpu.VMEM)],
        out_specs=pl.BlockSpec(memory_space=pltpu.VMEM),
        out_shape=jax.ShapeDtypeStruct(shape, jnp.float32),
        scratch_shapes=[
            pltpu.VMEM((sections, BLOCK, BLOCK), jnp.bfloat16),
            pltpu.VMEM((sections, 2, LAGS, columns * 8, BLOCK), jnp.float32),
            pltpu.VMEM((sections, columns * 8, BLOCK), jnp.float32),
        ],
        compiler_params=pltpu.CompilerParams(vmem_limit_bytes=16 * 1024 * 1024),
        cost_estimate=pl.CostEstimate(
            flops=4 * columns * pairs * BLOCK**3, bytes_accessed=2 * blocks.size, transcendentals=0
        ),
        name="scores",
    )(blocks)


def body(raw_sections, shift_rows, source_cols):
    raw = raw_sections[0]
    rows = lax.axis_size("row")
    sections = lax.axis_size("sec")
    own = lax.all_to_all(
        raw.reshape(rows, BLOCK, raw.shape[1]), "row", split_axis=0, concat_axis=0, tiled=True
    )
    chips = rows // 2
    links = [(2 * r, 2 * r - 1) for r in range(1, chips)]
    links += [(2 * r + 1, 2 * r + 2) for r in range(chips - 1)]
    across = lax.ppermute(own, "row", links)
    beside = lax.ppermute(own, "row", [(i, i ^ 1) for i in range(rows)])
    warped = warp(shift_rows[0, 0], source_cols[0, 0], own, beside, across)
    warped = warped.reshape(sections, -1, BLOCK, BLOCK)
    chunk = lax.all_to_all(warped, "sec", split_axis=0, concat_axis=0, tiled=True)
    result = scores(chunk)
    result = lax.all_to_all(result, "sec", split_axis=0, concat_axis=0, tiled=True)
    result = result.transpose(1, 2, 0, 3, 4).reshape(2, 1, LAGS, 1, -1, BLOCK)
    return result[0], result[1]


def solution(mesh):
    return jax.shard_map(
        body,
        mesh=mesh,
        in_specs=(P("sec", None, "row"), P("sec", "row", None), P("sec", "row", None)),
        out_specs=(P("sec", None, "row", None, None), P("sec", None, "row", None, None)),
        check_vma=False,
    )
```

```python
import functools

import jax
import jax.numpy as jnp
from jax import lax
from jax.experimental import pallas as pl
from jax.experimental.pallas import tpu as pltpu
from jax.sharding import PartitionSpec as P

BLOCK = 128
LAGS = 3
FIRST = 32


def warp_kernel(shifts, columns, own, beside, across, *outs, first):
    width = own.shape[2] // BLOCK
    toward = 2 * lax.rem(lax.axis_index("row"), 2) - 1
    rows = slice(first, first + across.shape[1])
    for away, out in enumerate(outs):
        begin = (lax.axis_index("sec") ^ away) * out.shape[0] if len(outs) > 1 else 0

        @pl.loop(0, out.shape[0], unroll=8)
        def _(near):
            column = columns[begin + near]
            stripe = lax.div(column, width)
            lane = pl.multiple_of(lax.rem(column, width) * BLOCK, BLOCK)
            side = shifts[begin + near] * toward
            here = own[stripe, rows, pl.ds(lane, BLOCK)]
            low = beside[stripe, rows, pl.ds(lane, BLOCK)]
            high = across[stripe, :, pl.ds(lane, BLOCK)]
            out[near] = jnp.where(side == 0, here, jnp.where(side == 1, high, low))


def warp(shifts, columns, own, beside, across, first, pieces, flops):
    shape = (shifts.shape[0] // pieces, across.shape[1], BLOCK)
    return pl.pallas_call(
        functools.partial(warp_kernel, first=first),
        in_specs=[pl.BlockSpec(memory_space=pltpu.SMEM)] * 2
        + [pl.BlockSpec(memory_space=pltpu.VMEM)] * 3,
        out_specs=[pl.BlockSpec(memory_space=pltpu.VMEM)] * pieces,
        out_shape=[jax.ShapeDtypeStruct(shape, jnp.bfloat16)] * pieces,
        compiler_params=pltpu.CompilerParams(vmem_limit_bytes=16 * 1024 * 1024),
        cost_estimate=pl.CostEstimate(
            flops=flops, bytes_accessed=8 * across.size, transcendentals=0
        ),
        name="warp",
    )(shifts, columns, own, beside, across)


def partial_lags(matrix):
    total = matrix[0:8]
    for start in range(8, matrix.shape[0], 8):
        total = total + pltpu.roll(matrix[start : start + 8], BLOCK - start, axis=1)
    return total


def halves(block):
    return jnp.concatenate([block[: BLOCK // 2], block[BLOCK // 2 :]], axis=1)


def turned(block):
    half = BLOCK // 2
    return jnp.concatenate([block, jnp.concatenate([block[half:], block[:half]], axis=0)], axis=1)


def along_lanes(left, right):
    return lax.dot_general(
        left, right, (((1,), (1,)), ((), ())), preferred_element_type=jnp.float32
    )


def score_kernel(high, *refs):
    sections, columns, rest = high.shape[:3]
    lows, refs = refs[:sections], refs[sections:]
    out, blocks, flipped, lags, squares = refs
    cut = BLOCK - rest
    half = BLOCK // 2
    me = lax.axis_index("sec")
    for away, low in enumerate(lows):
        blocks[me ^ away, :, :cut] = low[...]
    blocks[:, :, cut:] = high[...]
    for column in range(columns):
        place = slice(column * 8, (column + 1) * 8)
        for s in range(sections):
            block = blocks[s, column]
            flipped[s] = block.T
            values = block.astype(jnp.float32)
            values = values * values
            total = values[0:8]
            for start in range(8, BLOCK, 8):
                total = total + values[start : start + 8]
            squares[s, place, :] = total
        for back in range(sections - 1):
            count = min(LAGS, sections - 1 - back)
            near = range(back + 1, back + 1 + count)
            current = jnp.concatenate([halves(blocks[s, column]) for s in near], axis=0)
            current_flipped = jnp.concatenate([halves(flipped[s]) for s in near], axis=0)
            row_corr = along_lanes(current, turned(blocks[back, column]))
            col_corr = along_lanes(current_flipped, turned(flipped[back]))
            for k in range(count):
                part = slice(k * half, (k + 1) * half)
                lags[back + 1 + k, 0, k, place, :] = partial_lags(row_corr[part])
                lags[back + 1 + k, 1, k, place, :] = partial_lags(col_corr[part])
    energies = []
    for s in range(sections):
        total = squares[s, pl.ds(0, columns, stride=8), :]
        for b in range(1, 8):
            total = total + squares[s, pl.ds(b, columns, stride=8), :]
        energies.append(jnp.sum(total, axis=1, keepdims=True) / (BLOCK * BLOCK))
    for s in range(sections):
        for k in range(1, LAGS + 1):
            if s < k:
                for way in range(2):
                    out[s, way, k - 1] = jnp.zeros((columns, BLOCK), jnp.float32)
                continue
            scaling = 1.0 / (BLOCK * jnp.sqrt(energies[s] * energies[s - k] + 1e-06))
            for way in range(2):
                total = lags[s, way, k - 1, pl.ds(0, columns, stride=8), :]
                for b in range(1, 8):
                    row = lags[s, way, k - 1, pl.ds(b, columns, stride=8), :]
                    total = total + pltpu.roll(row, BLOCK - b, axis=1)
                out[s, way, k - 1] = total * scaling


def scores(lows, high):
    sections, columns = high.shape[:2]
    shape = (sections, 2, LAGS, columns, BLOCK)
    pairs = LAGS * sections - LAGS * (LAGS + 1) // 2
    return pl.pallas_call(
        score_kernel,
        in_specs=[pl.BlockSpec(memory_space=pltpu.VMEM)] * (1 + sections),
        out_specs=pl.BlockSpec(memory_space=pltpu.VMEM),
        out_shape=jax.ShapeDtypeStruct(shape, jnp.float32),
        scratch_shapes=[
            pltpu.VMEM((sections, columns, BLOCK, BLOCK), jnp.bfloat16),
            pltpu.VMEM((sections, BLOCK, BLOCK), jnp.bfloat16),
            pltpu.VMEM((sections, 2, LAGS, columns * 8, BLOCK), jnp.float32),
            pltpu.VMEM((sections, columns * 8, BLOCK), jnp.float32),
        ],
        compiler_params=pltpu.CompilerParams(vmem_limit_bytes=16 * 1024 * 1024),
        cost_estimate=pl.CostEstimate(
            flops=4 * columns * pairs * BLOCK**3, bytes_accessed=4 * high.size, transcendentals=0
        ),
        name="scores",
    )(high, *lows)


def body(raw_sections, shift_rows, source_cols):
    raw = raw_sections[0]
    rows = lax.axis_size("row")
    sections = lax.axis_size("sec")
    own = lax.all_to_all(
        raw.reshape(rows, BLOCK, raw.shape[1]), "row", split_axis=0, concat_axis=0, tiled=True
    )
    chips = rows // 2
    links = [(2 * r, 2 * r - 1) for r in range(1, chips)]
    links += [(2 * r + 1, 2 * r + 2) for r in range(chips - 1)]
    shifts, columns = shift_rows[0, 0], source_cols[0, 0]
    near = lax.ppermute(own[:, :FIRST], "row", links)
    far = lax.ppermute(own[:, FIRST:], "row", links)
    beside = lax.ppermute(own, "row", [(i, i ^ 1) for i in range(rows)])

    lows = warp(shifts, columns, own, beside, near, 0, sections, 12000000000)
    lows = [
        part if away == 0 else lax.ppermute(part, "sec", [(i, i ^ away) for i in range(sections)])
        for away, part in enumerate(lows)
    ]
    shifts, lows = lax.optimization_barrier((shifts, lows))
    (high,) = warp(shifts, columns, own, beside, far, FIRST, 1, 0)
    high = high.reshape(sections, -1, BLOCK - FIRST, BLOCK)
    high = lax.all_to_all(high, "sec", split_axis=0, concat_axis=0, tiled=True)
    result = scores(lows, high)
    result = lax.all_to_all(result, "sec", split_axis=0, concat_axis=0, tiled=True)
    result = result.transpose(1, 2, 0, 3, 4).reshape(2, 1, LAGS, 1, -1, BLOCK)
    return result[0], result[1]


def solution(mesh):
    return jax.shard_map(
        body,
        mesh=mesh,
        in_specs=(P("sec", None, "row"), P("sec", "row", None), P("sec", "row", None)),
        out_specs=(P("sec", None, "row", None, None), P("sec", None, "row", None, None)),
        check_vma=False,
    )
```

```python
import functools

import jax
import jax.numpy as jnp
from jax import lax
from jax.experimental import pallas as pl
from jax.experimental.pallas import tpu as pltpu
from jax.sharding import PartitionSpec as P

BLOCK = 128
LAGS = 3
FIRST = 16


def warp_kernel(shifts, columns, own, beside, across, *outs, first):
    width = own.shape[2] // BLOCK
    toward = 2 * lax.rem(lax.axis_index("row"), 2) - 1
    rows = slice(first, first + across.shape[1])
    for away, out in enumerate(outs):
        begin = (lax.axis_index("sec") ^ away) * out.shape[0] if len(outs) > 1 else 0

        @pl.loop(0, out.shape[0], unroll=8)
        def _(near):
            column = columns[begin + near]
            stripe = lax.div(column, width)
            lane = pl.multiple_of(lax.rem(column, width) * BLOCK, BLOCK)
            side = shifts[begin + near] * toward
            here = own[stripe, rows, pl.ds(lane, BLOCK)]
            low = beside[stripe, rows, pl.ds(lane, BLOCK)]
            high = across[stripe, :, pl.ds(lane, BLOCK)]
            out[near] = jnp.where(side == 0, here, jnp.where(side == 1, high, low))


def warp(shifts, columns, own, beside, across, first, pieces, flops):
    shape = (shifts.shape[0] // pieces, across.shape[1], BLOCK)
    return pl.pallas_call(
        functools.partial(warp_kernel, first=first),
        in_specs=[pl.BlockSpec(memory_space=pltpu.SMEM)] * 2
        + [pl.BlockSpec(memory_space=pltpu.VMEM)] * 3,
        out_specs=[pl.BlockSpec(memory_space=pltpu.VMEM)] * pieces,
        out_shape=[jax.ShapeDtypeStruct(shape, jnp.bfloat16)] * pieces,
        compiler_params=pltpu.CompilerParams(vmem_limit_bytes=16 * 1024 * 1024),
        cost_estimate=pl.CostEstimate(
            flops=flops, bytes_accessed=8 * across.size, transcendentals=0
        ),
        name="warp",
    )(shifts, columns, own, beside, across)


def partial_lags(matrix):
    total = matrix[0:8]
    for start in range(8, matrix.shape[0], 8):
        total = total + pltpu.roll(matrix[start : start + 8], BLOCK - start, axis=1)
    return total


def halves(block):
    return jnp.concatenate([block[: BLOCK // 2], block[BLOCK // 2 :]], axis=1)


def turned(block):
    half = BLOCK // 2
    return jnp.concatenate([block, jnp.concatenate([block[half:], block[:half]], axis=0)], axis=1)


def along_lanes(left, right):
    return lax.dot_general(
        left, right, (((1,), (1,)), ((), ())), preferred_element_type=jnp.float32
    )


def score_kernel(high, *refs):
    sections, columns, rest = high.shape[:3]
    lows, refs = refs[:sections], refs[sections:]
    out, blocks, flipped, lags, squares = refs
    cut = BLOCK - rest
    half = BLOCK // 2
    me = lax.axis_index("sec")
    for away, low in enumerate(lows):
        blocks[me ^ away, :, :cut] = low[...]
    blocks[:, :, cut:] = high[...]
    for column in range(columns):
        place = slice(column * 8, (column + 1) * 8)
        for s in range(sections):
            block = blocks[s, column]
            flipped[s] = block.T
            values = block.astype(jnp.float32)
            values = values * values
            total = values[0:8]
            for start in range(8, BLOCK, 8):
                total = total + values[start : start + 8]
            squares[s, place, :] = total
        for back in range(sections - 1):
            count = min(LAGS, sections - 1 - back)
            near = range(back + 1, back + 1 + count)
            current = jnp.concatenate([halves(blocks[s, column]) for s in near], axis=0)
            current_flipped = jnp.concatenate([halves(flipped[s]) for s in near], axis=0)
            row_corr = along_lanes(current, turned(blocks[back, column]))
            col_corr = along_lanes(current_flipped, turned(flipped[back]))
            for k in range(count):
                part = slice(k * half, (k + 1) * half)
                lags[back + 1 + k, 0, k, place, :] = partial_lags(row_corr[part])
                lags[back + 1 + k, 1, k, place, :] = partial_lags(col_corr[part])
    energies = []
    for s in range(sections):
        total = squares[s, pl.ds(0, columns, stride=8), :]
        for b in range(1, 8):
            total = total + squares[s, pl.ds(b, columns, stride=8), :]
        energies.append(jnp.sum(total, axis=1, keepdims=True) / (BLOCK * BLOCK))
    for s in range(sections):
        for k in range(1, LAGS + 1):
            if s < k:
                for way in range(2):
                    out[s, way, k - 1] = jnp.zeros((columns, BLOCK), jnp.float32)
                continue
            scaling = 1.0 / (BLOCK * jnp.sqrt(energies[s] * energies[s - k] + 1e-06))
            for way in range(2):
                total = lags[s, way, k - 1, pl.ds(0, columns, stride=8), :]
                for b in range(1, 8):
                    row = lags[s, way, k - 1, pl.ds(b, columns, stride=8), :]
                    total = total + pltpu.roll(row, BLOCK - b, axis=1)
                out[s, way, k - 1] = total * scaling


def scores(lows, high):
    sections, columns = high.shape[:2]
    shape = (sections, 2, LAGS, columns, BLOCK)
    pairs = LAGS * sections - LAGS * (LAGS + 1) // 2
    return pl.pallas_call(
        score_kernel,
        in_specs=[pl.BlockSpec(memory_space=pltpu.VMEM)] * (1 + sections),
        out_specs=pl.BlockSpec(memory_space=pltpu.VMEM),
        out_shape=jax.ShapeDtypeStruct(shape, jnp.float32),
        scratch_shapes=[
            pltpu.VMEM((sections, columns, BLOCK, BLOCK), jnp.bfloat16),
            pltpu.VMEM((sections, BLOCK, BLOCK), jnp.bfloat16),
            pltpu.VMEM((sections, 2, LAGS, columns * 8, BLOCK), jnp.float32),
            pltpu.VMEM((sections, columns * 8, BLOCK), jnp.float32),
        ],
        compiler_params=pltpu.CompilerParams(vmem_limit_bytes=16 * 1024 * 1024),
        cost_estimate=pl.CostEstimate(
            flops=4 * columns * pairs * BLOCK**3, bytes_accessed=4 * high.size, transcendentals=0
        ),
        name="scores",
    )(high, *lows)


def body(raw_sections, shift_rows, source_cols):
    raw = raw_sections[0]
    rows = lax.axis_size("row")
    sections = lax.axis_size("sec")
    own = lax.all_to_all(
        raw.reshape(rows, BLOCK, raw.shape[1]), "row", split_axis=0, concat_axis=0, tiled=True
    )
    chips = rows // 2
    links = [(2 * r, 2 * r - 1) for r in range(1, chips)]
    links += [(2 * r + 1, 2 * r + 2) for r in range(chips - 1)]
    shifts, columns = shift_rows[0, 0], source_cols[0, 0]
    near = lax.ppermute(own[:, :FIRST], "row", links)
    far = lax.ppermute(own[:, FIRST:], "row", links)
    beside = lax.ppermute(own, "row", [(i, i ^ 1) for i in range(rows)])

    lows = warp(shifts, columns, own, beside, near, 0, sections, 60000000000)
    lows = [
        part if away == 0 else lax.ppermute(part, "sec", [(i, i ^ away) for i in range(sections)])
        for away, part in enumerate(lows)
    ]
    shifts, lows = lax.optimization_barrier((shifts, lows))
    (high,) = warp(shifts, columns, own, beside, far, FIRST, 1, 0)
    high = high.reshape(sections, -1, BLOCK - FIRST, BLOCK)
    high = lax.all_to_all(high, "sec", split_axis=0, concat_axis=0, tiled=True)
    result = scores(lows, high)
    result = lax.all_to_all(result, "sec", split_axis=0, concat_axis=0, tiled=True)
    result = result.transpose(1, 2, 0, 3, 4).reshape(2, 1, LAGS, 1, -1, BLOCK)
    return result[0], result[1]


def solution(mesh):
    return jax.shard_map(
        body,
        mesh=mesh,
        in_specs=(P("sec", None, "row"), P("sec", "row", None), P("sec", "row", None)),
        out_specs=(P("sec", None, "row", None, None), P("sec", None, "row", None, None)),
        check_vma=False,
    )
```
